1024 devices in a mesh: blk: 64 (over y_lo, z), depth: 16 (over x, y_hi, core).
Axes of the slice: x: 4, y: 4 (y_hi: 2, y_lo: 2; y = y_hi * 2 + y_lo), z: 32, core: 2. Of those that a mesh axis runs over, the one named last changes fastest.
Arguments:
- video: bfloat16 [32768, 1152], P('blk'), may hold values from -0.1875 to 0.1875
- text: bfloat16 [32768, 1152], P(('blk', 'depth')), may hold values from -0.1875 to 0.1875
- video_ids: int32 [32768], P('blk'), may hold values from 0 to 511
- text_ids: int32 [32768], P(('blk', 'depth')), may hold values from 0 to 511
- log_scale: float32 [1], replicated, may hold values from 1.5 to 2.5
- bias: float32 [1], replicated, may hold values from -8 to -4
Outputs:
- loss: float32 [], replicated
- grad_video: float32 [32768, 1152], P(('blk', 'depth'))
- grad_text: float32 [32768, 1152], P(('blk', 'depth'))
The draws below stay inside these ranges and needn't reach their ends.
All inputs are finite; a program needn't handle non-finite values.
Results may differ from the reference program's by a relative error of at most 0.00095.
The reference program's roundings to bfloat16 on the way (of `coef`) count: a program that leaves them out, or rounds other values in their place, can miss the bound.
Values may be sent and summed in bfloat16 or wider, within the bound.
No kernel may reach another device: no remote copies, remote signals or barrier semaphores. Data moves between devices by JAX's collectives and lax.ppermute only.
A program may use at most 32 MiB of HBM per device.

```python
import jax
import jax.numpy as jnp
from jax import lax

D = 1152
ROWS_DEV = 512
CLIPS = 32768
N_BLK = 64


def place_ends(result, stream_key, smallest, high):
    place = [jax.random.randint(jax.random.fold_in(stream_key, axis), (), 0, length) for axis, length in enumerate(result.shape)]
    longest = result.shape.index(max(result.shape))
    next_to = place[:longest] + [(place[longest] + 1) % result.shape[longest]] + place[longest + 1:]
    return result.at[tuple(place)].set(smallest).at[tuple(next_to)].set(high)


def steps_of(key, dims, pieces, smallest, high):
    level, own = 1.0, jax.random.fold_in(key, 6)
    for axis_at, blocks in pieces:
        draws = jnp.exp(jax.random.uniform(jax.random.fold_in(own, axis_at), (blocks,), jnp.float32, smallest / len(pieces), high / len(pieces)))
        level = level * jnp.repeat(draws, dims[axis_at] // blocks).reshape([-1 if axis == axis_at else 1 for axis in range(len(dims))])
    return level


def scatter_about(stream_key, shape, deviation, bound, shards=(), kind=jnp.bfloat16):
    entries = jax.random.normal(stream_key, shape, jnp.float32) * deviation
    if len(shards) > 0:
        entries = steps_of(stream_key, shape, shards, -0.22, 0.18) * entries
    return jnp.clip(entries, min=-bound, max=bound).astype(kind)


def setup_inputs(seed: int = 0) -> dict:
    key_list = jax.random.split(jax.random.key(seed), 7)
    return {
        "video": scatter_about(key_list[0], (CLIPS, D), 0.03, 0.1875, ((0, 64),)),
        "text": scatter_about(key_list[1], (CLIPS, D), 0.03, 0.1875, ((0, 1024),)),
        "video_ids": place_ends(jax.random.randint(key_list[2], (CLIPS,), 0, ROWS_DEV), jax.random.fold_in(key_list[2], 1), 0, ROWS_DEV - 1).astype(jnp.int32),
        "text_ids": place_ends(jax.random.randint(key_list[3], (CLIPS,), 0, ROWS_DEV), jax.random.fold_in(key_list[3], 1), 0, ROWS_DEV - 1).astype(jnp.int32),
        "log_scale": jnp.clip(jax.random.uniform(key_list[4], (1,), jnp.float32, 1.5, 2.5), 1.5, 2.5),
        "bias": jnp.clip(jax.random.uniform(key_list[5], (1,), jnp.float32, -8.0, -4.0), -8.0, -4.0),
    }


EPS = 1e-06

def unit_rows(x):
    x32 = x.astype(jnp.float32)
    norms = jnp.sqrt(lax.optimization_barrier(jnp.sum(x32 * x32, axis=-1, keepdims=True)) + EPS)
    return (x32 / norms, norms)

def reference(video, text, video_ids, text_ids, log_scale, bias):
    vunit, vnorm = unit_rows(video)
    tunit, tnorm = unit_rows(text)
    vhat = vunit.astype(jnp.bfloat16).astype(jnp.float32)
    that = tunit.astype(jnp.bfloat16).astype(jnp.float32)
    scale = jnp.exp(log_scale[0])
    nblk = N_BLK
    half = nblk // 8
    vblocks = vhat.reshape(nblk, ROWS_DEV, D)
    vid_blocks = video_ids.reshape(nblk, ROWS_DEV)

    def one_offset(carry, offset):
        grad_v, grad_t, total = carry
        moved = (offset * ROWS_DEV).astype(jnp.int32)
        tblocks = jnp.roll(that, -moved, axis=0).reshape(nblk, ROWS_DEV, D)
        tid_blocks = jnp.roll(text_ids, -moved, axis=0).reshape(nblk, ROWS_DEV)
        dots = jnp.einsum('nrd,ncd->nrc', vblocks, tblocks, precision=lax.Precision.HIGHEST)
        logits = scale * dots + bias[0]
        sign = jnp.where(vid_blocks[:, :, None] == tid_blocks[:, None, :], 1.0, -1.0).astype(jnp.float32)
        total = total + jnp.sum(jax.nn.softplus(-sign * logits))
        coef = (-sign * jax.nn.sigmoid(-sign * logits) * scale).astype(jnp.bfloat16).astype(jnp.float32)
        grad_v = grad_v + jnp.einsum('nrc,ncd->nrd', coef, tblocks, precision=lax.Precision.HIGHEST).reshape(CLIPS, D)
        rolled = jnp.einsum('nrc,nrd->ncd', coef, vblocks, precision=lax.Precision.HIGHEST).reshape(CLIPS, D)
        grad_t = grad_t + jnp.roll(rolled, moved, axis=0)
        return ((grad_v, grad_t, total), None)
    offsets = jnp.arange(2 * half, dtype=jnp.int32) - (half - 1)
    start = (jnp.zeros((CLIPS, D), jnp.float32), jnp.zeros((CLIPS, D), jnp.float32), jnp.zeros((), jnp.float32))
    (grad_v, grad_t, total), _ = lax.scan(one_offset, start, offsets)
    loss = total / (CLIPS * 2 * half)
    grad_video = (grad_v - vunit * lax.optimization_barrier(jnp.sum(vunit * grad_v, axis=-1, keepdims=True))) / vnorm
    grad_text = (grad_t - tunit * lax.optimization_barrier(jnp.sum(tunit * grad_t, axis=-1, keepdims=True))) / tnorm
    return (loss, grad_video, grad_text)
```

```python
import jax
import jax.numpy as jnp
from jax import lax
from jax.experimental import pallas as pl
from jax.experimental.pallas import tpu as pltpu
from jax.sharding import PartitionSpec as P

EPS = 1e-06
LANES = 128
ID_BASE = 32
BF16 = jnp.bfloat16
F16 = jnp.float16
F32 = jnp.float32
CENTERS = (0, 3, -3, 6, -6)


def passed_along(value, steps):
    count = lax.axis_size("blk")
    pairs = [(source, (source + steps) % count) for source in range(count)]
    return lax.ppermute(value, "blk", pairs)


def unit_rows(x):
    x32 = x.astype(F32)
    norms = jnp.sqrt(jnp.sum(x32 * x32, axis=-1, keepdims=True) + EPS)
    return (x32 / norms, norms)


def coef_kernel(width, params, text_ref, vhat_ref, vids_ref, coef_ref, loss_ref):
    scale, bias = (params[0], params[1])
    marks = text_ref[:, width : width + LANES].astype(F32)
    tids = marks[:, 0:1] * ID_BASE + marks[:, 1:2]
    dots = lax.dot_general(
        text_ref[:, :width],
        vhat_ref[...],
        (((1,), (1,)), ((), ())),
        preferred_element_type=F32,
    )
    logits = scale * dots + bias
    flip = jnp.where(tids == vids_ref[...], -1.0, 1.0)
    z = flip * logits
    e = jnp.exp(-jnp.abs(z))
    losses = jnp.maximum(z, 0.0) + jnp.log1p(e)
    sig = jnp.where(z >= 0, 1.0, e) / (1.0 + e)
    coef_ref[...] = (flip * sig * scale).astype(BF16)
    loss_ref[...] = jnp.sum(losses, axis=0, keepdims=True)


def pair_coefs(params, text, vhat, vids):
    rows, width = vhat.shape
    vmem = pl.BlockSpec(memory_space=pltpu.VMEM)
    return pl.pallas_call(
        lambda *refs: coef_kernel(width, *refs),
        out_shape=(
            jax.ShapeDtypeStruct((text.shape[0], rows), BF16),
            jax.ShapeDtypeStruct((1, rows), F32),
        ),
        in_specs=[pl.BlockSpec(memory_space=pltpu.SMEM), vmem, vmem, vmem],
        out_specs=(vmem, vmem),
        compiler_params=pltpu.CompilerParams(vmem_limit_bytes=24 * 1024 * 1024),
        cost_estimate=pl.CostEstimate(
            flops=2 * text.shape[0] * rows * width,
            bytes_accessed=2 * width * (text.shape[0] + rows),
            transcendentals=3 * text.shape[0] * rows,
        ),
    )(params, text, vhat, vids)


def shards(video, text, video_ids, text_ids, log_scale, bias):
    rows, width = video.shape
    slice_rows = text.shape[0]
    nblk = lax.axis_size("blk")
    ndepth = lax.axis_size("depth")
    half = nblk // 8

    tunit, tnorm = unit_rows(text)
    digits = jnp.stack([text_ids // ID_BASE, text_ids % ID_BASE], axis=1).astype(BF16)
    digits = jnp.pad(digits, ((0, 0), (0, LANES - 2)))
    own = jnp.concatenate([tunit.astype(BF16), digits], axis=1)

    far_up = passed_along(own, -6)
    far_down = passed_along(own, 6)
    up = passed_along(own, -3)
    down = passed_along(own, 3)

    vunit, vnorm = unit_rows(video)
    vhat = vunit.astype(BF16)
    vids = video_ids.astype(F32)[None, :]
    params = jnp.stack([jnp.exp(log_scale[0]), bias[0]])

    bundle = jnp.concatenate([own, up, down, far_up, far_down], axis=0)
    above = passed_along(bundle, -1)
    below = passed_along(bundle, 1)
    last = passed_along(far_up, -2)

    def text_grad(coef):
        return jnp.einsum("cr,rd->cd", coef, vhat, preferred_element_type=F32)

    coef0, loss0 = pair_coefs(params, bundle, vhat, vids)
    grad0 = text_grad(coef0)
    arrived = jnp.concatenate([above, below, last], axis=0)
    coef1, loss1 = pair_coefs(params, arrived, vhat, vids)
    n = bundle.shape[0]
    back_up = passed_along(text_grad(coef1[:n]).astype(F16), 1)
    back_down = passed_along(text_grad(coef1[n : 2 * n]).astype(F16), -1)
    back_last = passed_along(text_grad(coef1[2 * n :]).astype(F16), 2)

    total = jnp.sum(loss0 + loss1)
    total = jnp.full((ndepth, LANES), total)
    total = jnp.sum(lax.all_to_all(total, "depth", 0, 0, tiled=True)[:, 0])
    total = jnp.full((nblk, LANES), total)
    total = jnp.sum(lax.all_to_all(total, "blk", 0, 0, tiled=True)[:, 0])
    loss = total / (rows * nblk * 2 * half)

    coefs = jnp.concatenate([coef0, coef1], axis=0)
    texts = jnp.concatenate([bundle, arrived], axis=0)[:, :width]
    share = jnp.einsum("cr,cd->rd", coefs, texts, preferred_element_type=F32)
    shares = lax.all_to_all(share.astype(F16), "depth", 0, 0, tiled=True)
    grad_vhat = jnp.sum(shares.reshape(ndepth, slice_rows, width).astype(F32), axis=0)

    held = grad0 + back_up.astype(F32) + back_down.astype(F32)
    held = held.reshape(len(CENTERS), slice_rows, width)
    held6 = held[3] + back_last.astype(F32)
    home = [passed_along(held6.astype(F16), 6), passed_along(held[4].astype(F16), -6)]
    home += [passed_along(held[1].astype(F16), 3), passed_along(held[2].astype(F16), -3)]
    grad_that = held[0] + sum(part.astype(F32) for part in home)

    offset = lax.axis_index("depth") * slice_rows
    own_unit, own_norm = unit_rows(lax.dynamic_slice_in_dim(video, offset, slice_rows, 0))
    grad_video = (
        grad_vhat - own_unit * jnp.sum(own_unit * grad_vhat, axis=-1, keepdims=True)
    ) / own_norm
    grad_text = (
        grad_that - tunit * jnp.sum(tunit * grad_that, axis=-1, keepdims=True)
    ) / tnorm
    return (loss, grad_video, grad_text)


def solution(mesh):
    placed = (P("blk", None), P(("blk", "depth"), None), P("blk"), P(("blk", "depth")), P(), P())
    return jax.shard_map(
        shards,
        mesh=mesh,
        in_specs=placed,
        out_specs=(P(), P(("blk", "depth"), None), P(("blk", "depth"), None)),
        check_vma=False,
    )
```

```python
import jax
import jax.numpy as jnp
from jax import lax
from jax.experimental import pallas as pl
from jax.experimental.pallas import tpu as pltpu
from jax.sharding import PartitionSpec as P

EPS = 1e-06
LANES = 128
ID_BASE = 32
BF16 = jnp.bfloat16
F16 = jnp.float16
F32 = jnp.float32


def passed_along(value, steps):
    count = lax.axis_size("blk")
    pairs = [(source, (source + steps) % count) for source in range(count)]
    return lax.ppermute(value, "blk", pairs)


def unit_rows(x):
    x32 = x.astype(F32)
    norms = jnp.sqrt(jnp.sum(x32 * x32, axis=-1, keepdims=True) + EPS)
    return (x32 / norms, norms)


def coef_kernel(width, params, text_ref, vhat_ref, vids_ref, coef_ref, loss_ref):
    scale, bias = (params[0], params[1])
    marks = text_ref[:, width : width + LANES].astype(F32)
    tids = marks[:, 0:1] * ID_BASE + marks[:, 1:2]
    dots = lax.dot_general(
        text_ref[:, :width],
        vhat_ref[...],
        (((1,), (1,)), ((), ())),
        preferred_element_type=F32,
    )
    logits = scale * dots + bias
    flip = jnp.where(tids == vids_ref[...], -1.0, 1.0)
    z = flip * logits
    e = jnp.exp(-jnp.abs(z))
    losses = jnp.maximum(z, 0.0) + jnp.log1p(e)
    sig = jnp.where(z >= 0, 1.0, e) / (1.0 + e)
    coef_ref[...] = (flip * sig * scale).astype(BF16)
    loss_ref[...] = jnp.sum(losses, axis=0, keepdims=True)


def pair_coefs(params, text, vhat, vids):
    rows, width = vhat.shape
    vmem = pl.BlockSpec(memory_space=pltpu.VMEM)
    return pl.pallas_call(
        lambda *refs: coef_kernel(width, *refs),
        out_shape=(
            jax.ShapeDtypeStruct((text.shape[0], rows), BF16),
            jax.ShapeDtypeStruct((1, rows), F32),
        ),
        in_specs=[pl.BlockSpec(memory_space=pltpu.SMEM), vmem, vmem, vmem],
        out_specs=(vmem, vmem),
        compiler_params=pltpu.CompilerParams(vmem_limit_bytes=24 * 1024 * 1024),
        cost_estimate=pl.CostEstimate(
            flops=2 * text.shape[0] * rows * width,
            bytes_accessed=2 * width * (text.shape[0] + rows),
            transcendentals=3 * text.shape[0] * rows,
        ),
    )(params, text, vhat, vids)


def own_kernel(width, text_ref, ids_ref, own_ref):
    x32 = text_ref[...].astype(F32)
    norms = jnp.sqrt(jnp.sum(x32 * x32, axis=-1, keepdims=True) + EPS)
    own_ref[:, :width] = (x32 / norms).astype(BF16)
    n = text_ref.shape[0]
    row = lax.broadcasted_iota(jnp.int32, (n, n), 0)
    col = lax.broadcasted_iota(jnp.int32, (n, n), 1)
    ids = jnp.sum(jnp.where(row == col, ids_ref[...], 0.0), axis=1, keepdims=True)
    high = jnp.floor(ids / ID_BASE)
    lane = lax.broadcasted_iota(jnp.int32, (n, LANES), 1)
    digits = jnp.where(lane == 0, high, ids - ID_BASE * high)
    own_ref[:, width:] = digits.astype(BF16)


def own_unit_slice(text, ids):
    n, width = text.shape
    vmem = pl.BlockSpec(memory_space=pltpu.VMEM)
    return pl.pallas_call(
        lambda *refs: own_kernel(width, *refs),
        out_shape=jax.ShapeDtypeStruct((n, width + LANES), BF16),
        in_specs=[vmem, vmem],
        out_specs=vmem,
    )(text, ids.astype(F32)[None, :])


def shards(video, text, video_ids, text_ids, log_scale, bias):
    rows, width = video.shape
    n = text.shape[0]
    nblk = lax.axis_size("blk")
    ndepth = lax.axis_size("depth")
    half = nblk // 8

    own = own_unit_slice(text, text_ids)
    up5 = passed_along(own, -5)
    down4 = passed_along(own, 4)

    vunit, _ = unit_rows(video)
    vhat = vunit.astype(BF16)
    vids = video_ids.astype(F32)[None, :]
    params = jnp.stack([jnp.exp(log_scale[0]), bias[0]])

    up27 = passed_along(jnp.concatenate([own, up5], axis=0), -2)
    down26 = passed_along(jnp.concatenate([own, down4], axis=0), 2)
    ups = passed_along(jnp.concatenate([own, up27, up5], axis=0), -1)
    downs = passed_along(jnp.concatenate([own, down4, down26, up5], axis=0), 1)

    def text_grad(coef):
        return jnp.einsum("cr,rd->cd", coef, vhat, preferred_element_type=F32)

    held_text = jnp.concatenate([own, up27, up5, down4, down26], axis=0)
    arrived = jnp.concatenate([ups, downs], axis=0)
    coef0, loss0 = pair_coefs(params, held_text, vhat, vids)
    coef1, loss1 = pair_coefs(params, arrived, vhat, vids)

    total = jnp.sum(loss0 + loss1) / (rows * nblk * 2 * half)
    total = jnp.full((nblk, LANES), total)
    total = jnp.sum(lax.all_to_all(total, "blk", 0, 0, tiled=True)[:, 0])

    held = text_grad(coef0)
    back_up = passed_along(text_grad(coef1[: 4 * n]).astype(F16), 1)
    back_down = passed_along(text_grad(coef1[4 * n :]).astype(F16), -1)

    coefs = jnp.concatenate([coef0, coef1], axis=0)
    texts = jnp.concatenate([held_text, arrived], axis=0)
    share = jnp.einsum("cr,cd->rd", coefs, texts, preferred_element_type=F32).astype(F16)
    first = total.astype(F16)
    rest = (total - first.astype(F32)) * 2.0**11
    second = rest.astype(F16)
    third = ((rest - second.astype(F32)) * 2.0**11).astype(F16)
    lane = lax.broadcasted_iota(jnp.int32, (rows, LANES), 1)
    digits = jnp.where(lane == 0, first, jnp.where(lane == 1, second, third))
    share = lax.dynamic_update_slice(share, digits, (0, width))
    shares = lax.all_to_all(share, "depth", 0, 0, tiled=True)
    shares = shares.reshape(ndepth, n, width + LANES)
    grad_vhat = jnp.sum(shares[:, :, :width].astype(F32), axis=0)
    digits = jnp.sum(shares[:, 0, width : width + 3].astype(F32), axis=0)
    loss = digits[0] + digits[1] * 2.0**-11 + digits[2] * 2.0**-22

    held = held.reshape(7, n, width)
    back_up = back_up.astype(F32).reshape(4, n, width)
    back_down = back_down.astype(F32).reshape(5, n, width)
    to_up = held[1:3] + back_up[1:3]
    to_down = held[5:7] + back_down[2:4]
    home5 = held[3] + back_up[3] + back_down[4]
    home4 = held[4] + back_down[1]
    home = held[0] + back_up[0] + back_down[0]
    back_up = passed_along(to_up.astype(F16), 2).astype(F32)
    back_down = passed_along(to_down.astype(F16), -2).astype(F32)
    home5 = passed_along((home5 + back_up[1]).astype(F16), 5)
    home4 = passed_along((home4 + back_down[1]).astype(F16), -4)
    home = home + back_up[0] + back_down[0]
    grad_that = home + home5.astype(F32) + home4.astype(F32)

    tunit, tnorm = unit_rows(text)
    offset = lax.axis_index("depth") * n
    own_unit, own_norm = unit_rows(lax.dynamic_slice_in_dim(video, offset, n, 0))
    grad_video = (
        grad_vhat - own_unit * jnp.sum(own_unit * grad_vhat, axis=-1, keepdims=True)
    ) / own_norm
    grad_text = (
        grad_that - tunit * jnp.sum(tunit * grad_that, axis=-1, keepdims=True)
    ) / tnorm
    return (loss, grad_video, grad_text)


def solution(mesh):
    placed = (P("blk", None), P(("blk", "depth"), None), P("blk"), P(("blk", "depth")), P(), P())
    return jax.shard_map(
        shards,
        mesh=mesh,
        in_specs=placed,
        out_specs=(P(), P(("blk", "depth"), None), P(("blk", "depth"), None)),
        check_vma=False,
    )
```

```python
import jax
import jax.numpy as jnp
from jax import lax
from jax.experimental import pallas as pl
from jax.experimental.pallas import tpu as pltpu
from jax.sharding import PartitionSpec as P

EPS = 1e-06
LANES = 128
ID_BASE = 32
BF16 = jnp.bfloat16
F16 = jnp.float16
F32 = jnp.float32


def passed_along(value, steps):
    count = lax.axis_size("blk")
    pairs = [(source, (source + steps) % count) for source in range(count)]
    return lax.ppermute(value, "blk", pairs)


def unit_rows(x):
    x32 = x.astype(F32)
    norms = jnp.sqrt(jnp.sum(x32 * x32, axis=-1, keepdims=True) + EPS)
    return (x32 / norms, norms)


def coef_kernel(width, params, text_ref, vhat_ref, vids_ref, before_ref, coef_ref, loss_ref):
    scale, bias, part = (params[0], params[1], params[2])
    marks = text_ref[:, width : width + LANES].astype(F32)
    tids = marks[:, 0:1] * ID_BASE + marks[:, 1:2]
    dots = lax.dot_general(
        text_ref[:, :width],
        vhat_ref[...],
        (((1,), (1,)), ((), ())),
        preferred_element_type=F32,
    )
    logits = scale * dots + bias
    flip = jnp.where(tids == vids_ref[...], -1.0, 1.0)
    z = flip * logits
    e = jnp.exp(-jnp.abs(z))
    losses = jnp.maximum(z, 0.0) + jnp.log1p(e)
    sig = jnp.where(z >= 0, 1.0, e) / (1.0 + e)
    coef_ref[...] = (flip * sig * scale).astype(BF16)
    total = jnp.sum(losses, axis=0, keepdims=True)
    total = jnp.sum(total, axis=1, keepdims=True) * part
    loss_ref[...] = before_ref[...] + total


def pair_coefs(params, text, vhat, vids, before):
    rows, width = vhat.shape
    vmem = pl.BlockSpec(memory_space=pltpu.VMEM)
    return pl.pallas_call(
        lambda *refs: coef_kernel(width, *refs),
        out_shape=(
            jax.ShapeDtypeStruct((text.shape[0], rows), BF16),
            jax.ShapeDtypeStruct(before.shape, F32),
        ),
        in_specs=[pl.BlockSpec(memory_space=pltpu.SMEM), vmem, vmem, vmem, vmem],
        out_specs=(vmem, vmem),
        compiler_params=pltpu.CompilerParams(vmem_limit_bytes=24 * 1024 * 1024),
        cost_estimate=pl.CostEstimate(
            flops=2 * text.shape[0] * rows * width,
            bytes_accessed=2 * width * (text.shape[0] + rows),
            transcendentals=3 * text.shape[0] * rows,
        ),
    )(params, text, vhat, vids, before)


def own_kernel(width, text_ref, ids_ref, own_ref):
    x32 = text_ref[...].astype(F32)
    norms = jnp.sqrt(jnp.sum(x32 * x32, axis=-1, keepdims=True) + EPS)
    own_ref[:, :width] = (x32 / norms).astype(BF16)
    n = text_ref.shape[0]
    row = lax.broadcasted_iota(jnp.int32, (n, n), 0)
    col = lax.broadcasted_iota(jnp.int32, (n, n), 1)
    ids = jnp.where(row == col, ids_ref[...].astype(F32), 0.0)
    ids = jnp.sum(ids, axis=1, keepdims=True)
    high = jnp.floor(ids / ID_BASE)
    lane = lax.broadcasted_iota(jnp.int32, (n, LANES), 1)
    digits = jnp.where(lane == 0, high, ids - ID_BASE * high)
    own_ref[:, width:] = digits.astype(BF16)


def own_unit_slice(text, ids):
    n, width = text.shape
    vmem = pl.BlockSpec(memory_space=pltpu.VMEM)
    return pl.pallas_call(
        lambda *refs: own_kernel(width, *refs),
        out_shape=jax.ShapeDtypeStruct((n, width + LANES), BF16),
        in_specs=[vmem, vmem],
        out_specs=vmem,
    )(text, ids[None, :])


def exchanged(value, side):
    count = lax.axis_size("blk")
    pairs = [(b, (b + (1 if (b + side) % 2 == 0 else -1)) % count) for b in range(count)]
    return lax.ppermute(value, "blk", pairs)


def shards(video, text, video_ids, text_ids, log_scale, bias):
    rows, width = video.shape
    n = text.shape[0]
    nblk = lax.axis_size("blk")
    ndepth = lax.axis_size("depth")
    half = nblk // 8
    even = lax.axis_index("blk") % 2 == 0

    own = own_unit_slice(text, text_ids)
    up5 = passed_along(own, -5)
    down4 = passed_along(own, 4)

    vunit, _ = unit_rows(video)
    vhat = vunit.astype(BF16)
    vids = video_ids.astype(F32)[None, :]
    part = jnp.float32(1.0 / (rows * nblk * 2 * half))
    params = jnp.stack([jnp.exp(log_scale[0]), bias[0], part])

    up27 = passed_along(jnp.concatenate([own, up5], axis=0), -2)
    down26 = passed_along(jnp.concatenate([own, down4], axis=0), 2)
    for_lower = jnp.concatenate([own, up27[:n], up5, up27[n:], up5], axis=0)
    for_upper = jnp.concatenate([own, down4, down26, up5], axis=0)
    side0 = exchanged(jnp.where(even, for_upper, for_lower), 0)
    side1 = exchanged(jnp.where(even, for_lower, for_upper), 1)

    def text_grad(coef):
        return jnp.einsum("cr,rd->cd", coef, vhat, preferred_element_type=F32)

    def video_grad(coef, texts):
        return jnp.einsum("cr,cd->rd", coef, texts, preferred_element_type=F32)

    held_text = jnp.concatenate([own, up27, up5, down4, down26], axis=0)
    coef0, total = pair_coefs(params, held_text, vhat, vids, jnp.zeros((nblk, LANES), F32))
    share0 = video_grad(coef0, held_text)
    held = text_grad(coef0)

    fifth = jnp.where(even, side1[4 * n :], side0[4 * n :])
    arrived = jnp.concatenate([side0[: 4 * n], side1[: 4 * n], fifth], axis=0)
    coef1, total = pair_coefs(params, arrived, vhat, vids, total)

    coef_side0 = jnp.concatenate([coef1[: 4 * n], coef1[8 * n :]], axis=0)
    back0 = exchanged(text_grad(coef_side0).astype(F16), 0)
    back1 = exchanged(text_grad(coef1[4 * n :]).astype(F16), 1)

    share = (share0 + video_grad(coef1, arrived)).astype(F16)
    share, total = lax.optimization_barrier((share, total))
    totals = lax.all_to_all(total, "blk", 0, 0, tiled=True)

    def unit_of(value, i):
        return value[i * n : (i + 1) * n].astype(F32)

    def of_sides(i, j):
        low = jnp.where(even, unit_of(back1, i), unit_of(back0, i)) if i is not None else 0.0
        high = jnp.where(even, unit_of(back0, j), unit_of(back1, j)) if j is not None else 0.0
        return low + high

    to_up = [unit_of(held, 1) + of_sides(1, None), unit_of(held, 2) + of_sides(3, None)]
    to_down = [unit_of(held, 5) + of_sides(None, 2), unit_of(held, 6) + of_sides(None, 3)]
    back_up = passed_along(jnp.concatenate(to_up, axis=0).astype(F16), 2)
    back_down = passed_along(jnp.concatenate(to_down, axis=0).astype(F16), -2)
    totals, _, _ = lax.optimization_barrier((totals, back_up, back_down))
    total = jnp.sum(totals[:, 0])
    first = total.astype(F16)
    rest = (total - first.astype(F32)) * 2.0**11
    second = rest.astype(F16)
    third = ((rest - second.astype(F32)) * 2.0**11).astype(F16)
    lane = lax.broadcasted_iota(jnp.int32, (rows, LANES), 1)
    digits = jnp.where(lane == 0, first, jnp.where(lane == 1, second, third))
    share = lax.dynamic_update_slice(share, digits, (0, width))
    shares = lax.all_to_all(share, "depth", 0, 0, tiled=True)
    shares = shares.reshape(ndepth, n, width + LANES)
    grad_vhat = jnp.sum(shares[:, :, :width].astype(F32), axis=0)
    digits = jnp.sum(shares[:, 0, width : width + 3].astype(F32), axis=0)
    loss = digits[0] + digits[1] * 2.0**-11 + digits[2] * 2.0**-22

    home5 = unit_of(held, 3) + of_sides(2, 4) + unit_of(back_up, 1)
    home4 = unit_of(held, 4) + of_sides(None, 1) + unit_of(back_down, 1)
    home = unit_of(held, 0) + of_sides(0, 0) + unit_of(back_up, 0) + unit_of(back_down, 0)
    home5 = passed_along(home5.astype(F16), 5)
    home4 = passed_along(home4.astype(F16), -4)
    grad_that = home + home5.astype(F32) + home4.astype(F32)

    tunit, tnorm = unit_rows(text)
    offset = lax.axis_index("depth") * n
    own_unit, own_norm = unit_rows(lax.dynamic_slice_in_dim(video, offset, n, 0))
    grad_video = (
        grad_vhat - own_unit * jnp.sum(own_unit * grad_vhat, axis=-1, keepdims=True)
    ) / own_norm
    grad_text = (
        grad_that - tunit * jnp.sum(tunit * grad_that, axis=-1, keepdims=True)
    ) / tnorm
    return (loss, grad_video, grad_text)


def solution(mesh):
    placed = (P("blk", None), P(("blk", "depth"), None), P("blk"), P(("blk", "depth")), P(), P())
    return jax.shard_map(
        shards,
        mesh=mesh,
        in_specs=placed,
        out_specs=(P(), P(("blk", "depth"), None), P(("blk", "depth"), None)),
        check_vma=False,
    )
```

```python
import jax
import jax.numpy as jnp
from jax import lax
from jax.experimental import pallas as pl
from jax.experimental.pallas import tpu as pltpu
from jax.sharding import PartitionSpec as P

EPS = 1e-06
LANES = 128
ID_BASE = 32
BF16 = jnp.bfloat16
F16 = jnp.float16
F32 = jnp.float32


def passed_along(value, steps0, steps1):
    nblk, ndepth = (lax.axis_size("blk"), lax.axis_size("depth"))
    pairs = []
    for b in range(nblk):
        for d in range(ndepth):
            to = (b + (steps1 if d % 2 else steps0)) % nblk
            pairs.append((b * ndepth + d, to * ndepth + d))
    return lax.ppermute(value, ("blk", "depth"), pairs)


def core_swapped(value):
    ndepth = lax.axis_size("depth")
    return lax.ppermute(value, "depth", [(d, d ^ 1) for d in range(ndepth)])


def unit_rows(x):
    x32 = x.astype(F32)
    norms = jnp.sqrt(jnp.sum(x32 * x32, axis=-1, keepdims=True) + EPS)
    return (x32 / norms, norms)


def coef_kernel(width, params, text_ref, vhat_ref, vids_ref, before_ref, coef_ref, loss_ref):
    scale, bias, part = (params[0], params[1], params[2])
    marks = text_ref[:, width : width + LANES].astype(F32)
    tids = marks[:, 0:1] * ID_BASE + marks[:, 1:2]
    dots = lax.dot_general(
        text_ref[:, :width],
        vhat_ref[...],
        (((1,), (1,)), ((), ())),
        preferred_element_type=F32,
    )
    logits = scale * dots + bias
    flip = jnp.where(tids == vids_ref[...], -1.0, 1.0)
    z = flip * logits
    e = jnp.exp(-jnp.abs(z))
    losses = jnp.maximum(z, 0.0) + jnp.log1p(e)
    sig = jnp.where(z >= 0, 1.0, e) / (1.0 + e)
    coef_ref[...] = (flip * sig * scale).astype(BF16)
    total = jnp.sum(losses, axis=0, keepdims=True)
    total = jnp.sum(total, axis=1, keepdims=True) * part
    loss_ref[...] = before_ref[...] + total


def pair_coefs(params, text, vhat, vids, before):
    rows, width = vhat.shape
    vmem = pl.BlockSpec(memory_space=pltpu.VMEM)
    return pl.pallas_call(
        lambda *refs: coef_kernel(width, *refs),
        out_shape=(
            jax.ShapeDtypeStruct((text.shape[0], rows), BF16),
            jax.ShapeDtypeStruct(before.shape, F32),
        ),
        in_specs=[pl.BlockSpec(memory_space=pltpu.SMEM), vmem, vmem, vmem, vmem],
        out_specs=(vmem, vmem),
        compiler_params=pltpu.CompilerParams(vmem_limit_bytes=24 * 1024 * 1024),
        cost_estimate=pl.CostEstimate(
            flops=2 * text.shape[0] * rows * width,
            bytes_accessed=2 * width * (text.shape[0] + rows),
            transcendentals=3 * text.shape[0] * rows,
        ),
    )(params, text, vhat, vids, before)


def own_kernel(width, text_ref, ids_ref, own_ref):
    x32 = text_ref[...].astype(F32)
    norms = jnp.sqrt(jnp.sum(x32 * x32, axis=-1, keepdims=True) + EPS)
    own_ref[:, :width] = (x32 / norms).astype(BF16)
    n = text_ref.shape[0]
    row = lax.broadcasted_iota(jnp.int32, (n, n), 0)
    col = lax.broadcasted_iota(jnp.int32, (n, n), 1)
    ids = jnp.where(row == col, ids_ref[...].astype(F32), 0.0)
    ids = jnp.sum(ids, axis=1, keepdims=True)
    high = jnp.floor(ids / ID_BASE)
    lane = lax.broadcasted_iota(jnp.int32, (n, LANES), 1)
    digits = jnp.where(lane == 0, high, ids - ID_BASE * high)
    own_ref[:, width:] = digits.astype(BF16)


def own_unit_slice(text, ids):
    n, width = text.shape
    vmem = pl.BlockSpec(memory_space=pltpu.VMEM)
    return pl.pallas_call(
        lambda *refs: own_kernel(width, *refs),
        out_shape=jax.ShapeDtypeStruct((n, width + LANES), BF16),
        in_specs=[vmem, vmem],
        out_specs=vmem,
    )(text, ids[None, :])


def shards(video, text, video_ids, text_ids, log_scale, bias):
    rows, width = video.shape
    n = text.shape[0]
    nblk = lax.axis_size("blk")
    ndepth = lax.axis_size("depth")
    half = nblk // 8
    depth = lax.axis_index("depth")
    core0 = depth % 2 == 0

    own = own_unit_slice(text, text_ids)
    r1 = passed_along(own, -5, 4)
    r2 = passed_along(own, 4, -5)

    def by_core(x):
        x = x.reshape(ndepth // 2, 2, n, *x.shape[1:])
        mine = jnp.where(core0, x[:, 0], x[:, 1])
        other = jnp.where(core0, x[:, 1], x[:, 0])
        return jnp.stack([mine, other]).reshape(rows, *x.shape[3:])

    vunit, _ = unit_rows(by_core(video))
    vhat = vunit.astype(BF16)
    vids = by_core(video_ids).astype(F32)[None, :]
    part = jnp.float32(1.0 / (rows * nblk * 2 * half))
    params = jnp.stack([jnp.exp(log_scale[0]), bias[0], part])

    q1 = passed_along(jnp.concatenate([own, r1], axis=0), -2, 2)
    q2 = passed_along(jnp.concatenate([own, r2], axis=0), 2, -2)
    s1 = passed_along(jnp.concatenate([own, q1, r1, r2], axis=0), -1, 1)
    s2 = passed_along(jnp.concatenate([own, q2, r2, r1], axis=0), 1, -1)

    def text_grad(coef):
        return jnp.einsum("cr,rd->cd", coef, vhat, preferred_element_type=F32)

    def video_grad(coef, texts):
        return jnp.einsum("cr,cd->rd", coef, texts, preferred_element_type=F32)

    held_text = jnp.concatenate([own, q1, r1, q2, r2], axis=0)
    coef0, total = pair_coefs(params, held_text, vhat, vids, jnp.zeros((nblk, LANES), F32))
    share0 = video_grad(coef0, held_text)
    held = text_grad(coef0)
    s1, s2, share0, held = lax.optimization_barrier((s1, s2, share0, held))

    fifth = jnp.where(core0, s2[4 * n :], s1[4 * n :])
    arrived = jnp.concatenate([s1[: 4 * n], s2[: 4 * n], fifth], axis=0)
    coef1, total = pair_coefs(params, arrived, vhat, vids, total)

    total = total + core_swapped(total)
    totals = lax.all_to_all(total, "blk", 0, 0, tiled=True)

    coef_s1 = jnp.concatenate([coef1[: 4 * n], coef1[8 * n :]], axis=0)
    m1 = passed_along(text_grad(coef_s1).astype(F16), 1, -1)
    m2 = passed_along(text_grad(coef1[4 * n :]).astype(F16), -1, 1)
    m1, m2, _ = lax.optimization_barrier((m1, m2, total))

    mid = rows // 2
    sent = (share0[mid:] + video_grad(coef1[:, mid:], arrived)).astype(F16)
    share = share0[:mid] + video_grad(coef1[:, :mid], arrived)
    share = (share + core_swapped(sent).astype(F32)).astype(F16)

    def unit_of(value, i):
        return value[i * n : (i + 1) * n].astype(F32)

    def pair_of(i, back):
        units = [unit_of(held, i) + unit_of(back, 1), unit_of(held, i + 1) + unit_of(back, 2)]
        return jnp.concatenate(units, axis=0).astype(F16)

    n1 = passed_along(pair_of(1, m1), 2, -2)
    n2 = passed_along(pair_of(4, m2), -2, 2)

    totals, _, _ = lax.optimization_barrier((totals, n1, n2))
    total = jnp.sum(totals[:, 0])
    first = total.astype(F16)
    rest = (total - first.astype(F32)) * 2.0**11
    second = rest.astype(F16)
    third = ((rest - second.astype(F32)) * 2.0**11).astype(F16)
    lane = lax.broadcasted_iota(jnp.int32, (mid, LANES), 1)
    digits = jnp.where(lane == 0, first, jnp.where(lane == 1, second, third))
    share = lax.dynamic_update_slice(share, digits, (0, width))
    groups = [list(range(core, ndepth, 2)) for core in range(2)]
    shares = lax.all_to_all(share, "depth", 0, 0, axis_index_groups=groups, tiled=True)
    shares = shares.reshape(ndepth // 2, n, width + LANES)
    grad_vhat = jnp.sum(shares[:, :, :width].astype(F32), axis=0)
    digits = jnp.sum(shares[:, 0, width : width + 3].astype(F32), axis=0)
    loss = digits[0] + digits[1] * 2.0**-11 + digits[2] * 2.0**-22

    h1 = unit_of(held, 3) + unit_of(m1, 3) + jnp.where(core0, unit_of(m2, 4), 0.0) + unit_of(n1, 1)
    h2 = unit_of(held, 6) + unit_of(m2, 3) + jnp.where(core0, 0.0, unit_of(m1, 4)) + unit_of(n2, 1)
    home = unit_of(held, 0) + unit_of(m1, 0) + unit_of(m2, 0) + unit_of(n1, 0) + unit_of(n2, 0)
    h1 = passed_along(h1.astype(F16), 5, -4)
    h2 = passed_along(h2.astype(F16), -4, 5)
    grad_that = home + h1.astype(F32) + h2.astype(F32)

    tunit, tnorm = unit_rows(text)
    own_unit, own_norm = unit_rows(lax.dynamic_slice_in_dim(video, depth * n, n, 0))
    grad_video = (
        grad_vhat - own_unit * jnp.sum(own_unit * grad_vhat, axis=-1, keepdims=True)
    ) / own_norm
    grad_text = (
        grad_that - tunit * jnp.sum(tunit * grad_that, axis=-1, keepdims=True)
    ) / tnorm
    return (loss, grad_video, grad_text)


def solution(mesh):
    placed = (P("blk", None), P(("blk", "depth"), None), P("blk"), P(("blk", "depth")), P(), P())
    return jax.shard_map(
        shards,
        mesh=mesh,
        in_specs=placed,
        out_specs=(P(), P(("blk", "depth"), None), P(("blk", "depth"), None)),
        check_vma=False,
    )
```

```python
import jax
import jax.numpy as jnp
from jax import lax
from jax.experimental import pallas as pl
from jax.experimental.pallas import tpu as pltpu
from jax.sharding import PartitionSpec as P

EPS = 1e-06
LANES = 128
ID_BASE = 32
BF16 = jnp.bfloat16
F16 = jnp.float16
F32 = jnp.float32


def passed_along(value, steps0, steps1):
    nblk, ndepth = (lax.axis_size("blk"), lax.axis_size("depth"))
    pairs = []
    for b in range(nblk):
        for d in range(ndepth):
            to = (b + (steps1 if d % 2 else steps0)) % nblk
            pairs.append((b * ndepth + d, to * ndepth + d))
    return lax.ppermute(value, ("blk", "depth"), pairs)


def core_swapped(value):
    ndepth = lax.axis_size("depth")
    return lax.ppermute(value, "depth", [(d, d ^ 1) for d in range(ndepth)])


def unit_rows(x):
    x32 = x.astype(F32)
    norms = jnp.sqrt(jnp.sum(x32 * x32, axis=-1, keepdims=True) + EPS)
    return (x32 / norms, norms)


def coef_kernel(width, params, text_ref, vhat_ref, vids_ref, before_ref, coef_ref, loss_ref):
    scale, bias, part = (params[0], params[1], params[2])
    marks = text_ref[:, width : width + LANES].astype(F32)
    tids = marks[:, 0:1] * ID_BASE + marks[:, 1:2]
    dots = lax.dot_general(
        text_ref[:, :width],
        vhat_ref[...],
        (((1,), (1,)), ((), ())),
        preferred_element_type=F32,
    )
    logits = scale * dots + bias
    flip = jnp.where(tids == vids_ref[...], -1.0, 1.0)
    z = flip * logits
    e = jnp.exp(-jnp.abs(z))
    losses = jnp.maximum(z, 0.0) + jnp.log1p(e)
    sig = jnp.where(z >= 0, 1.0, e) / (1.0 + e)
    coef_ref[...] = (flip * sig * scale).astype(BF16)
    total = jnp.sum(losses, axis=0, keepdims=True)
    total = jnp.sum(total, axis=1, keepdims=True) * part
    loss_ref[...] = before_ref[...] + total


def pair_coefs(params, text, vhat, vids, before):
    rows, width = vhat.shape
    vmem = pl.BlockSpec(memory_space=pltpu.VMEM)
    return pl.pallas_call(
        lambda *refs: coef_kernel(width, *refs),
        out_shape=(
            jax.ShapeDtypeStruct((text.shape[0], rows), BF16),
            jax.ShapeDtypeStruct(before.shape, F32),
        ),
        in_specs=[pl.BlockSpec(memory_space=pltpu.SMEM), vmem, vmem, vmem, vmem],
        out_specs=(vmem, vmem),
        compiler_params=pltpu.CompilerParams(vmem_limit_bytes=24 * 1024 * 1024),
        cost_estimate=pl.CostEstimate(
            flops=2 * text.shape[0] * rows * width,
            bytes_accessed=2 * width * (text.shape[0] + rows),
            transcendentals=3 * text.shape[0] * rows,
        ),
    )(params, text, vhat, vids, before)


def own_kernel(width, text_ref, ids_ref, own_ref):
    x32 = text_ref[...].astype(F32)
    norms = jnp.sqrt(jnp.sum(x32 * x32, axis=-1, keepdims=True) + EPS)
    own_ref[:, :width] = (x32 / norms).astype(BF16)
    n = text_ref.shape[0]
    row = lax.broadcasted_iota(jnp.int32, (n, n), 0)
    col = lax.broadcasted_iota(jnp.int32, (n, n), 1)
    ids = jnp.where(row == col, ids_ref[...].astype(F32), 0.0)
    ids = jnp.sum(ids, axis=1, keepdims=True)
    high = jnp.floor(ids / ID_BASE)
    lane = lax.broadcasted_iota(jnp.int32, (n, LANES), 1)
    digits = jnp.where(lane == 0, high, ids - ID_BASE * high)
    own_ref[:, width:] = digits.astype(BF16)


def own_unit_slice(text, ids):
    n, width = text.shape
    vmem = pl.BlockSpec(memory_space=pltpu.VMEM)
    return pl.pallas_call(
        lambda *refs: own_kernel(width, *refs),
        out_shape=jax.ShapeDtypeStruct((n, width + LANES), BF16),
        in_specs=[vmem, vmem],
        out_specs=vmem,
    )(text, ids[None, :])


def shards(video, text, video_ids, text_ids, log_scale, bias):
    rows, width = video.shape
    n = text.shape[0]
    nblk = lax.axis_size("blk")
    ndepth = lax.axis_size("depth")
    half = nblk // 8
    depth = lax.axis_index("depth")
    core0 = depth % 2 == 0

    own = own_unit_slice(text, text_ids)
    r1 = passed_along(own, -5, 4)
    r2 = passed_along(own, 4, -5)

    video32 = video.astype(F32)
    vnorm = jnp.sqrt(jnp.sum(video32 * video32, axis=-1, keepdims=True) + EPS)
    vnorm, r1 = lax.optimization_barrier((vnorm, r1))
    vhat = (video32 / vnorm).astype(BF16)
    vids = video_ids.astype(F32)[None, :]
    part = jnp.float32(1.0 / (rows * nblk * 2 * half))
    params = jnp.stack([jnp.exp(log_scale[0]), bias[0], part])

    q1 = passed_along(jnp.concatenate([own, r1], axis=0), -2, 2)
    q2 = passed_along(jnp.concatenate([own, r2], axis=0), 2, -2)
    s1 = passed_along(jnp.concatenate([own, q1, r1, r2], axis=0), -1, 1)
    s2 = passed_along(jnp.concatenate([own, q2, r2, r1], axis=0), 1, -1)

    def text_grad(coef):
        return jnp.einsum("cr,rd->cd", coef, vhat, preferred_element_type=F32)

    def video_grad(coef, texts):
        return jnp.einsum("cr,cd->rd", coef, texts, preferred_element_type=F32)

    held_text = jnp.concatenate([own, q1, r1, q2, r2], axis=0)
    coef0, total = pair_coefs(params, held_text, vhat, vids, jnp.zeros((nblk, LANES), F32))
    share0 = video_grad(coef0, held_text)
    held = text_grad(coef0)
    s1, s2, share0, held = lax.optimization_barrier((s1, s2, share0, held))

    fifth = jnp.where(core0, s2[4 * n :], s1[4 * n :])
    arrived = jnp.concatenate([s1[: 4 * n], s2[: 4 * n], fifth], axis=0)
    coef1, total = pair_coefs(params, arrived, vhat, vids, total)

    totals = lax.all_to_all(total, "blk", 0, 0, tiled=True)

    coef_s1 = jnp.concatenate([coef1[: 4 * n], coef1[8 * n :]], axis=0)
    m1 = passed_along(text_grad(coef_s1).astype(F16), 1, -1)
    m2 = passed_along(text_grad(coef1[4 * n :]).astype(F16), -1, 1)

    share = (share0 + video_grad(coef1, arrived)).astype(F16)

    def unit_of(value, i):
        return value[i * n : (i + 1) * n].astype(F32)

    def pair_of(i, back):
        units = [unit_of(held, i) + unit_of(back, 1), unit_of(held, i + 1) + unit_of(back, 2)]
        return jnp.concatenate(units, axis=0).astype(F16)

    n1 = passed_along(pair_of(1, m1), 2, -2)
    n2 = passed_along(pair_of(4, m2), -2, 2)

    totals, _, _ = lax.optimization_barrier((totals, n1, n2))
    total = jnp.sum(totals, axis=0, keepdims=True)
    first = total.astype(F16)
    rest = (total - first.astype(F32)) * 2.0**11
    second = rest.astype(F16)
    third = ((rest - second.astype(F32)) * 2.0**11).astype(F16)
    lane = lax.broadcasted_iota(jnp.int32, (1, LANES), 1)
    digits = jnp.where(lane == 0, first, jnp.where(lane == 1, second, third))
    digits = jnp.broadcast_to(digits, (rows, LANES))
    share = lax.dynamic_update_slice(share, digits, (0, width))
    shares = lax.all_to_all(share, "depth", 0, 0, tiled=True).reshape(ndepth, n, width + LANES)
    grad_vhat = jnp.sum(shares[:, :, :width].astype(F32), axis=0)
    digits = jnp.sum(shares[:, 0, width : width + 3].astype(F32), axis=0)
    loss = digits[0] + digits[1] * 2.0**-11 + digits[2] * 2.0**-22

    h1 = unit_of(held, 3) + unit_of(m1, 3) + jnp.where(core0, unit_of(m2, 4), 0.0) + unit_of(n1, 1)
    h2 = unit_of(held, 6) + unit_of(m2, 3) + jnp.where(core0, 0.0, unit_of(m1, 4)) + unit_of(n2, 1)
    home = unit_of(held, 0) + unit_of(m1, 0) + unit_of(m2, 0) + unit_of(n1, 0) + unit_of(n2, 0)
    h1 = passed_along(h1.astype(F16), 5, -4)
    h2 = passed_along(h2.astype(F16), -4, 5)
    grad_that = home + h1.astype(F32) + h2.astype(F32)

    tunit, tnorm = unit_rows(text)
    own_unit, own_norm = unit_rows(lax.dynamic_slice_in_dim(video, depth * n, n, 0))
    grad_video = (
        grad_vhat - own_unit * jnp.sum(own_unit * grad_vhat, axis=-1, keepdims=True)
    ) / own_norm
    grad_text = (
        grad_that - tunit * jnp.sum(tunit * grad_that, axis=-1, keepdims=True)
    ) / tnorm
    return (loss, grad_video, grad_text)


def solution(mesh):
    placed = (P("blk", None), P(("blk", "depth"), None), P("blk"), P(("blk", "depth")), P(), P())
    return jax.shard_map(
        shards,
        mesh=mesh,
        in_specs=placed,
        out_specs=(P(), P(("blk", "depth"), None), P(("blk", "depth"), None)),
        check_vma=False,
    )
```

```python
import jax
import jax.numpy as jnp
from jax import lax
from jax.experimental import pallas as pl
from jax.experimental.pallas import tpu as pltpu
from jax.sharding import PartitionSpec as P

EPS = 1e-06
LANES = 128
ID_BASE = 32
BF16 = jnp.bfloat16
F16 = jnp.float16
F32 = jnp.float32


def moved(value, rule):
    nblk, ndepth = (lax.axis_size("blk"), lax.axis_size("depth"))
    pairs = []
    for b in range(nblk):
        for d in range(ndepth):
            to = rule(b, d)
            if to is not None:
                pairs.append((b * ndepth + d, to[0] % nblk * ndepth + to[1]))
    return lax.ppermute(value, ("blk", "depth"), pairs)


def passed_along(value, steps0, steps1):
    return moved(value, lambda b, d: (b + (steps1 if d % 2 else steps0), d))


def unit_rows(x):
    x32 = x.astype(F32)
    norms = jnp.sqrt(jnp.sum(x32 * x32, axis=-1, keepdims=True) + EPS)
    return (x32 / norms, norms)


def coef_kernel(width, params, text_ref, vhat_ref, vids_ref, before_ref, coef_ref, loss_ref):
    scale, bias, part = (params[0], params[1], params[2])
    marks = text_ref[:, width : width + LANES].astype(F32)
    tids = marks[:, 0:1] * ID_BASE + marks[:, 1:2]
    dots = lax.dot_general(
        text_ref[:, :width],
        vhat_ref[...],
        (((1,), (1,)), ((), ())),
        preferred_element_type=F32,
    )
    logits = scale * dots + bias
    flip = jnp.where(tids == vids_ref[...], -1.0, 1.0)
    z = flip * logits
    e = jnp.exp(-jnp.abs(z))
    losses = jnp.maximum(z, 0.0) + jnp.log1p(e)
    sig = jnp.where(z >= 0, 1.0, e) / (1.0 + e)
    coef_ref[...] = (flip * sig * scale).astype(BF16)
    total = jnp.sum(losses, axis=0, keepdims=True)
    total = jnp.sum(total, axis=1, keepdims=True) * part
    loss_ref[...] = before_ref[...] + total


def pair_coefs(params, text, vhat, vids, before):
    rows, width = vhat.shape
    vmem = pl.BlockSpec(memory_space=pltpu.VMEM)
    return pl.pallas_call(
        lambda *refs: coef_kernel(width, *refs),
        out_shape=(
            jax.ShapeDtypeStruct((text.shape[0], rows), BF16),
            jax.ShapeDtypeStruct(before.shape, F32),
        ),
        in_specs=[pl.BlockSpec(memory_space=pltpu.SMEM), vmem, vmem, vmem, vmem],
        out_specs=(vmem, vmem),
        compiler_params=pltpu.CompilerParams(vmem_limit_bytes=24 * 1024 * 1024),
        cost_estimate=pl.CostEstimate(
            flops=2 * text.shape[0] * rows * width,
            bytes_accessed=2 * width * (text.shape[0] + rows),
            transcendentals=3 * text.shape[0] * rows,
        ),
    )(params, text, vhat, vids, before)


def own_kernel(width, text_ref, ids_ref, own_ref):
    x32 = text_ref[...].astype(F32)
    norms = jnp.sqrt(jnp.sum(x32 * x32, axis=-1, keepdims=True) + EPS)
    own_ref[:, :width] = (x32 / norms).astype(BF16)
    n = text_ref.shape[0]
    row = lax.broadcasted_iota(jnp.int32, (n, n), 0)
    col = lax.broadcasted_iota(jnp.int32, (n, n), 1)
    ids = jnp.where(row == col, ids_ref[...].astype(F32), 0.0)
    ids = jnp.sum(ids, axis=1, keepdims=True)
    high = jnp.floor(ids / ID_BASE)
    lane = lax.broadcasted_iota(jnp.int32, (n, LANES), 1)
    digits = jnp.where(lane == 0, high, ids - ID_BASE * high)
    own_ref[:, width:] = digits.astype(BF16)


def own_unit_slice(text, ids):
    n, width = text.shape
    vmem = pl.BlockSpec(memory_space=pltpu.VMEM)
    return pl.pallas_call(
        lambda *refs: own_kernel(width, *refs),
        out_shape=jax.ShapeDtypeStruct((n, width + LANES), BF16),
        in_specs=[vmem, vmem],
        out_specs=vmem,
    )(text, ids[None, :])


def shards(video, text, video_ids, text_ids, log_scale, bias):
    rows, width = video.shape
    n = text.shape[0]
    nblk = lax.axis_size("blk")
    ndepth = lax.axis_size("depth")
    half = nblk // 8
    depth = lax.axis_index("depth")
    core0 = depth % 2 == 0

    own = own_unit_slice(text, text_ids)
    near = moved(own, lambda b, d: (b - 1, d - 1) if d % 2 else (b, d + 1))
    above = moved(own, lambda b, d: None if d % 2 else (b - 1, d))
    base = jnp.concatenate([jnp.where(core0, above, near), jnp.where(core0, near, own)], axis=0)

    video32 = video.astype(F32)
    vnorm = jnp.sqrt(jnp.sum(video32 * video32, axis=-1, keepdims=True) + EPS)
    vnorm, base = lax.optimization_barrier((vnorm, base))
    vhat = (video32 / vnorm).astype(BF16)
    vids = video_ids.astype(F32)[None, :]
    part = jnp.float32(1.0 / (rows * nblk * 2 * half))
    params = jnp.stack([jnp.exp(log_scale[0]), bias[0], part])

    by4 = passed_along(base, -4, 4)
    by2 = passed_along(jnp.concatenate([base, by4], axis=0), -2, 2)
    held_text = jnp.concatenate([base, by4, by2], axis=0)
    arrived = passed_along(held_text, -1, 1)

    def text_grad(coef):
        return jnp.einsum("cr,rd->cd", coef, vhat, preferred_element_type=F32)

    def video_grad(coef, texts):
        return jnp.einsum("cr,cd->rd", coef, texts, preferred_element_type=F32)

    coef0, total = pair_coefs(params, held_text, vhat, vids, jnp.zeros((nblk, LANES), F32))
    share0 = video_grad(coef0, held_text)
    held = text_grad(coef0)
    arrived, share0, held = lax.optimization_barrier((arrived, share0, held))
    coef1, total = pair_coefs(params, arrived, vhat, vids, total)

    back1 = passed_along(text_grad(coef1).astype(F16), 1, -1)

    totals = lax.all_to_all(total, "blk", 0, 0, tiled=True)

    share = (share0 + video_grad(coef1, arrived)).astype(F16)

    def rows_of(value, i, j):
        return value[i * n : j * n].astype(F32)

    back2 = passed_along((rows_of(held, 4, 8) + rows_of(back1, 4, 8)).astype(F16), 2, -2)
    home4 = rows_of(held, 2, 4) + rows_of(back1, 2, 4) + rows_of(back2, 2, 4)
    home = rows_of(held, 0, 2) + rows_of(back1, 0, 2) + rows_of(back2, 0, 2)
    home = home + passed_along(home4.astype(F16), 4, -4).astype(F32)

    to_near = jnp.where(core0, home[n:], home[:n]).astype(F16)
    near = moved(to_near, lambda b, d: (b, d - 1) if d % 2 else (b + 1, d + 1))
    below = moved(home[:n].astype(F16), lambda b, d: None if d % 2 else (b + 1, d))
    grad_that = near.astype(F32) + jnp.where(core0, below.astype(F32), home[n:])

    totals, back2 = lax.optimization_barrier((totals, back2))
    total = jnp.sum(totals, axis=0, keepdims=True)
    first = total.astype(F16)
    rest = (total - first.astype(F32)) * 2.0**11
    second = rest.astype(F16)
    third = ((rest - second.astype(F32)) * 2.0**11).astype(F16)
    lane = lax.broadcasted_iota(jnp.int32, (1, LANES), 1)
    digits = jnp.where(lane == 2, third, jnp.zeros_like(third))
    digits = jnp.where(lane == 0, first, jnp.where(lane == 1, second, digits))
    digits = jnp.broadcast_to(digits, (rows, LANES))
    share = lax.dynamic_update_slice(share, digits, (0, width))
    shares = lax.all_to_all(share, "depth", 0, 0, tiled=True).reshape(ndepth, n, width + LANES)
    grad_vhat = jnp.sum(shares[:, :, :width].astype(F32), axis=0)
    weight = jnp.where(lane == 0, 1.0, jnp.where(lane == 1, 2.0**-11, 2.0**-22))
    weight = jnp.where(lane < 3, weight, 0.0)
    loss = jnp.sum(shares[:, 0, width:].astype(F32) * weight)

    tunit, tnorm = unit_rows(text)
    own_norm = lax.dynamic_slice_in_dim(vnorm, depth * n, n, 0)
    own_unit = lax.dynamic_slice_in_dim(video, depth * n, n, 0).astype(F32) / own_norm
    grad_video = (
        grad_vhat - own_unit * jnp.sum(own_unit * grad_vhat, axis=-1, keepdims=True)
    ) / own_norm
    grad_text = (
        grad_that - tunit * jnp.sum(tunit * grad_that, axis=-1, keepdims=True)
    ) / tnorm
    return (loss, grad_video, grad_text)


def solution(mesh):
    placed = (P("blk", None), P(("blk", "depth"), None), P("blk"), P(("blk", "depth")), P(), P())
    return jax.shard_map(
        shards,
        mesh=mesh,
        in_specs=placed,
        out_specs=(P(), P(("blk", "depth"), None), P(("blk", "depth"), None)),
        check_vma=False,
    )
```

```python
import jax
import jax.numpy as jnp
from jax import lax
from jax.experimental import pallas as pl
from jax.experimental.pallas import tpu as pltpu
from jax.sharding import PartitionSpec as P

EPS = 1e-06
LANES = 128
ID_BASE = 32
BF16 = jnp.bfloat16
F16 = jnp.float16
F32 = jnp.float32


def moved(value, rule):
    nblk, ndepth = (lax.axis_size("blk"), lax.axis_size("depth"))
    pairs = []
    for b in range(nblk):
        for d in range(ndepth):
            to = rule(b, d)
            if to is not None:
                pairs.append((b * ndepth + d, to[0] % nblk * ndepth + to[1]))
    return lax.ppermute(value, ("blk", "depth"), pairs)


def passed_along(value, steps0, steps1):
    return moved(value, lambda b, d: (b + (steps1 if d % 2 else steps0), d))


def unit_rows(x):
    x32 = x.astype(F32)
    norms = jnp.sqrt(jnp.sum(x32 * x32, axis=-1, keepdims=True) + EPS)
    return (x32 / norms, norms)


def coef_kernel(width, params, text_ref, vhat_ref, vids_ref, before_ref, coef_ref, loss_ref):
    scale, bias, part = (params[0], params[1], params[2])
    marks = text_ref[:, width : width + LANES].astype(F32)
    tids = marks[:, 0:1] * ID_BASE + marks[:, 1:2]
    dots = lax.dot_general(
        text_ref[:, :width],
        vhat_ref[...],
        (((1,), (1,)), ((), ())),
        preferred_element_type=F32,
    )
    logits = scale * dots + bias
    flip = jnp.where(tids == vids_ref[...], -1.0, 1.0)
    z = flip * logits
    e = jnp.exp(-jnp.abs(z))
    losses = jnp.maximum(z, 0.0) + jnp.log1p(e)
    sig = jnp.where(z >= 0, 1.0, e) / (1.0 + e)
    coef_ref[...] = (flip * sig * scale).astype(BF16)
    total = jnp.sum(losses, axis=0, keepdims=True)
    total = jnp.sum(total, axis=1, keepdims=True) * part
    loss_ref[...] = before_ref[...] + total


def pair_coefs(params, text, vhat, vids, before):
    rows, width = vhat.shape
    vmem = pl.BlockSpec(memory_space=pltpu.VMEM)
    return pl.pallas_call(
        lambda *refs: coef_kernel(width, *refs),
        out_shape=(
            jax.ShapeDtypeStruct((text.shape[0], rows), BF16),
            jax.ShapeDtypeStruct(before.shape, F32),
        ),
        in_specs=[pl.BlockSpec(memory_space=pltpu.SMEM), vmem, vmem, vmem, vmem],
        out_specs=(vmem, vmem),
        compiler_params=pltpu.CompilerParams(vmem_limit_bytes=24 * 1024 * 1024),
        cost_estimate=pl.CostEstimate(
            flops=2 * text.shape[0] * rows * width,
            bytes_accessed=2 * width * (text.shape[0] + rows),
            transcendentals=3 * text.shape[0] * rows,
        ),
    )(params, text, vhat, vids, before)


def own_kernel(width, text_ref, ids_ref, own_ref):
    x32 = text_ref[...].astype(F32)
    norms = jnp.sqrt(jnp.sum(x32 * x32, axis=-1, keepdims=True) + EPS)
    own_ref[:, :width] = (x32 / norms).astype(BF16)
    n = text_ref.shape[0]
    row = lax.broadcasted_iota(jnp.int32, (n, n), 0)
    col = lax.broadcasted_iota(jnp.int32, (n, n), 1)
    ids = jnp.where(row == col, ids_ref[...].astype(F32), 0.0)
    ids = jnp.sum(ids, axis=1, keepdims=True)
    high = jnp.floor(ids / ID_BASE)
    lane = lax.broadcasted_iota(jnp.int32, (n, LANES), 1)
    digits = jnp.where(lane == 0, high, ids - ID_BASE * high)
    own_ref[:, width:] = digits.astype(BF16)


def own_unit_slice(text, ids):
    n, width = text.shape
    vmem = pl.BlockSpec(memory_space=pltpu.VMEM)
    return pl.pallas_call(
        lambda *refs: own_kernel(width, *refs),
        out_shape=jax.ShapeDtypeStruct((n, width + LANES), BF16),
        in_specs=[vmem, vmem],
        out_specs=vmem,
    )(text, ids[None, :])


def shards(video, text, video_ids, text_ids, log_scale, bias):
    rows, width = video.shape
    n = text.shape[0]
    nblk = lax.axis_size("blk")
    ndepth = lax.axis_size("depth")
    half = nblk // 8
    depth = lax.axis_index("depth")
    core0 = depth % 2 == 0

    own = own_unit_slice(text, text_ids)
    near = moved(own, lambda b, d: (b - 1, d - 1) if d % 2 else (b, d + 1))
    above = moved(own, lambda b, d: None if d % 2 else (b - 1, d))
    base = jnp.concatenate([jnp.where(core0, above, near), jnp.where(core0, near, own)], axis=0)

    video32 = video.astype(F32)
    vnorm = jnp.sqrt(jnp.sum(video32 * video32, axis=-1, keepdims=True) + EPS)
    vnorm, base = lax.optimization_barrier((vnorm, base))
    vhat = (video32 / vnorm).astype(BF16)
    vids = video_ids.astype(F32)[None, :]
    part = jnp.float32(1.0 / (rows * nblk * 2 * half))
    params = jnp.stack([jnp.exp(log_scale[0]), bias[0], part])

    by4 = passed_along(base, -4, 4)
    own_video = lax.dynamic_slice_in_dim(video, depth * n, n, 0)
    own_video, text, by4 = lax.optimization_barrier((own_video, text, by4))
    own_unit, own_norm = unit_rows(own_video)
    tunit, tnorm = unit_rows(text)
    by2 = passed_along(jnp.concatenate([base, by4], axis=0), -2, 2)
    held_text = jnp.concatenate([base, by4, by2], axis=0)
    arrived = passed_along(held_text, -1, 1)

    def text_grad(coef):
        return jnp.einsum("cr,rd->cd", coef, vhat, preferred_element_type=F32)

    def video_grad(coef, texts):
        return jnp.einsum("cr,cd->rd", coef, texts, preferred_element_type=F32)

    coef0, total = pair_coefs(params, held_text, vhat, vids, jnp.zeros((nblk, LANES), F32))
    share0 = video_grad(coef0, held_text)
    held = text_grad(coef0)
    arrived, share0, held, own_unit, own_norm, tunit, tnorm = lax.optimization_barrier(
        (arrived, share0, held, own_unit, own_norm, tunit, tnorm)
    )
    coef1, total = pair_coefs(params, arrived, vhat, vids, total)

    back1 = passed_along(text_grad(coef1).astype(F16), 1, -1)

    totals = lax.all_to_all(total, "blk", 0, 0, tiled=True)

    share = (share0 + video_grad(coef1, arrived)).astype(F16)

    def rows_of(value, i, j):
        return value[i * n : j * n].astype(F32)

    back2 = passed_along((rows_of(held, 4, 8) + rows_of(back1, 4, 8)).astype(F16), 2, -2)
    home4 = rows_of(held, 2, 4) + rows_of(back1, 2, 4) + rows_of(back2, 2, 4)
    home = rows_of(held, 0, 2) + rows_of(back1, 0, 2) + rows_of(back2, 0, 2)
    home = home + passed_along(home4.astype(F16), 4, -4).astype(F32)

    to_near = jnp.where(core0, home[n:], home[:n]).astype(F16)
    near = moved(to_near, lambda b, d: (b, d - 1) if d % 2 else (b + 1, d + 1))
    below = moved(home[:n].astype(F16), lambda b, d: None if d % 2 else (b + 1, d))
    grad_that = near.astype(F32) + jnp.where(core0, below.astype(F32), home[n:])

    totals, back2 = lax.optimization_barrier((totals, back2))
    total = jnp.sum(totals, axis=0, keepdims=True)
    first = total.astype(F16)
    rest = (total - first.astype(F32)) * 2.0**11
    second = rest.astype(F16)
    third = ((rest - second.astype(F32)) * 2.0**11).astype(F16)
    lane = lax.broadcasted_iota(jnp.int32, (1, LANES), 1)
    digits = jnp.where(lane == 2, third, jnp.zeros_like(third))
    digits = jnp.where(lane == 0, first, jnp.where(lane == 1, second, digits))
    digits = jnp.broadcast_to(digits, (rows, LANES))
    share = lax.dynamic_update_slice(share, digits, (0, width))
    shares = lax.all_to_all(share, "depth", 0, 0, tiled=True).reshape(ndepth, n, width + LANES)
    grad_vhat = jnp.sum(shares[:, :, :width].astype(F32), axis=0)
    weight = jnp.where(lane == 0, 1.0, jnp.where(lane == 1, 2.0**-11, 2.0**-22))
    weight = jnp.where(lane < 3, weight, 0.0)
    loss = jnp.sum(shares[:, 0, width:].astype(F32) * weight)

    grad_video = (
        grad_vhat - own_unit * jnp.sum(own_unit * grad_vhat, axis=-1, keepdims=True)
    ) / own_norm
    grad_text = (
        grad_that - tunit * jnp.sum(tunit * grad_that, axis=-1, keepdims=True)
    ) / tnorm
    return (loss, grad_video, grad_text)


def solution(mesh):
    placed = (P("blk", None), P(("blk", "depth"), None), P("blk"), P(("blk", "depth")), P(), P())
    return jax.shard_map(
        shards,
        mesh=mesh,
        in_specs=placed,
        out_specs=(P(), P(("blk", "depth"), None), P(("blk", "depth"), None)),
        check_vma=False,
    )
```
